256 devices in a mesh: dp: 8 (over y, z_hi), mp: 32 (over z_lo, x, core).
Axes of the slice: x: 4, y: 4, z: 8 (z_hi: 2, z_lo: 4; z = z_hi * 4 + z_lo), core: 2. Of those that a mesh axis runs over, the one named last changes fastest.
Arguments:
- tokens: bfloat16 [131072, 4096], P(('dp', 'mp')), may hold values from -170 to 170
- outgrads: bfloat16 [131072, 4096], P(('dp', 'mp')), may hold values from -11 to 11
- grad_parts: bfloat16 [8, 64, 512, 512], P('dp', 'mp'), may hold values from -6 to 6
- basis_slots: bfloat16 [32, 512, 512], P('mp'), may hold values from -0.25 to 0.25
- pattern: int32 [2, 8], replicated, may hold values from 0 to 7, each once within a row
- owners: int32 [16], replicated, may hold values from 0 to 31, as said below
Outputs:
- precond: bfloat16 [64, 512, 512], P('mp')
- eigenvalues: float32 [16, 512], replicated
The draws below stay inside these ranges and needn't reach their ends.
Inputs may be any that keep to these rules, and one draw needn't show every extreme that they name: `pattern`: each row is a permutation of 0 to 7. `owners`: the entries are distinct; 0 and 31 are always among them.
All inputs are finite; a program needn't handle non-finite values.
Results may differ from the reference program's by a relative error of at most 0.006.
Values may be sent and summed in bfloat16 or wider, within the bound.
A program may use at most 128 MiB of HBM per device.

```python
import math
import jax
import jax.numpy as jnp
from jax import lax

D = 4096
BS = 512
NB = 8
GROUPS = 8
SLOTS = 32
TOKENS = 131072


def scale_rows(key, entries, smallest, largest):
    row_count = entries.shape[0]
    spread = jnp.exp(jax.random.uniform(key, (row_count, 1), jnp.float32, math.log(smallest), math.log(largest)))
    rising = 0.5 + jnp.arange(row_count, dtype=jnp.float32)[:, None] / row_count
    return entries * spread * rising


def mix_columns(key, entries, off_scale):
    diag_key, off_key, column_key = jax.random.split(key, 3)
    blocks = entries.reshape(TOKENS, NB, BS)
    identity = jnp.eye(BS, dtype=jnp.float32)[None, :, :]
    diagonal = jax.random.uniform(diag_key, (NB, 1, BS), jnp.float32, 0.6, 1.4)
    spread = jnp.clip(jax.random.normal(off_key, (NB, BS, BS), jnp.float32), -4.0, 4.0)
    mixing = identity * diagonal + off_scale / math.sqrt(BS) * spread
    mixed = jnp.einsum('tbi,bij->tbj', blocks, mixing, precision=lax.Precision.HIGHEST)
    mixed = mixed / math.sqrt(1.0 + off_scale * off_scale)
    columns = jnp.exp(jax.random.uniform(column_key, (1, NB, BS), jnp.float32, math.log(0.5), math.log(2.0)))
    return (jnp.clip(mixed, -4.0, 4.0) * columns).reshape(TOKENS, D)


def draw_tokens(key, part):
    key = jax.random.fold_in(key, 11)
    first_key, second_key, third_key = jax.random.split(key, 3)
    entries = jnp.clip(jax.random.normal(first_key, (TOKENS, D), jnp.float32), -6.0, 6.0)
    mixed = mix_columns(third_key, entries, 1.2)
    return (4.0 * scale_rows(second_key, mixed, 0.3, 3.0)).astype(jnp.bfloat16)


def draw_outgrads(key, part):
    key = jax.random.fold_in(key, 23)
    first_key, second_key, third_key = jax.random.split(key, 3)
    entries = jnp.clip(jax.random.normal(first_key, (TOKENS, D), jnp.float32), -6.0, 6.0)
    mixed = mix_columns(third_key, entries, 1.2)
    return (0.25 * scale_rows(second_key, mixed, 0.3, 3.0)).astype(jnp.bfloat16)


def draw_owners(key, part):
    key = jax.random.fold_in(key, 5)
    first_key, second_key = jax.random.split(key, 2)
    middle = jax.random.permutation(first_key, SLOTS - 2).astype(jnp.int32) + 1
    ends = jnp.array([0, SLOTS - 1], dtype=jnp.int32)
    picked = jnp.concatenate([ends, middle[:2 * NB - 2]])
    return jax.random.permutation(second_key, picked).astype(jnp.int32)


def block_scale(rng, shape, shards, low, top_value):
    loudness = 1.0
    for dim, parts in shards:
        heights = jax.random.uniform(jax.random.fold_in(jax.random.fold_in(rng, 6), dim), (parts,), jnp.float32, low / len(shards), top_value / len(shards))
        loudness = loudness * jnp.repeat(jnp.exp(heights), shape[dim] // parts).reshape((-1,) + (1,) * (len(shape) - 1 - dim))
    return loudness


def centred(stream_key, shape, deviation, most, cuts=(), kind=jnp.bfloat16):
    factor_of = block_scale(stream_key, shape, cuts, -0.22, 0.18) if cuts else 1.0
    values = jax.random.normal(stream_key, shape, jnp.float32) * deviation * factor_of
    return jnp.minimum(jnp.maximum(values, -most), most).astype(kind)


def setup_inputs(seed: int = 0) -> dict:
    splits = jax.random.split(jax.random.key(seed), 7)
    return {
        "tokens": draw_tokens(jax.random.fold_in(splits[6], 71), 0),
        "outgrads": draw_outgrads(jax.random.fold_in(splits[6], 71), 0),
        "grad_parts": centred(splits[2], (GROUPS, NB * NB, BS, BS), 1.0, 6.0, ((0, 8), (1, 32))),
        "basis_slots": centred(splits[3], (SLOTS, BS, BS), BS ** -0.5, 0.25, ((0, 32),)),
        "pattern": jax.vmap(lambda own: jax.random.permutation(own, NB))(jax.random.split(splits[4], 2)).reshape((2, NB)).astype(jnp.int32),
        "owners": draw_owners(jax.random.fold_in(splits[6], 71), 0),
    }


DAMPING = 0.5


def inverse_order(placing):
    places = jnp.arange(placing.shape[0], dtype=jnp.int32)
    hits = (placing[:, None] == places[None, :]).astype(jnp.int32)
    return jnp.sum(places[:, None] * hits, axis=0).astype(jnp.int32)


def side_moments(values, placing, side_bases):
    blocks = values.reshape(values.shape[0], placing.shape[0], -1)

    def single(item_pair):
        position, block_basis = item_pair
        selected = lax.dynamic_index_in_dim(blocks, position, axis=1, keepdims=False)
        projected = jnp.dot(selected, block_basis, preferred_element_type=jnp.float32)
        return jnp.sum(projected * projected, axis=0)

    return lax.map(single, (placing, side_bases))


def precondition(gradient, out_basis, in_basis, out_scale, in_scale):
    contract = (((0,), (0,)), ((), ()))
    halfway = lax.dot_general(out_basis, gradient, contract, preferred_element_type=jnp.float32).astype(jnp.bfloat16)
    rotated = jnp.dot(halfway, in_basis, preferred_element_type=jnp.float32)
    scaled = (rotated / (out_scale[:, None] * in_scale[None, :] + DAMPING)).astype(jnp.bfloat16)
    returned = jnp.dot(out_basis, scaled, preferred_element_type=jnp.float32).astype(jnp.bfloat16)
    trailing = (((1,), (1,)), ((), ()))
    return lax.dot_general(returned, in_basis, trailing, preferred_element_type=jnp.float32).astype(jnp.bfloat16)


def reference(tokens, outgrads, grad_parts, basis_slots, pattern, owners):
    bases_used = jnp.take(basis_slots, owners, axis=0).reshape(2, NB, BS, BS)
    moments = jnp.stack([side_moments(outgrads, pattern[0], bases_used[0]),
                         side_moments(tokens, pattern[1], bases_used[1])])
    eigenvalues = moments / TOKENS
    summed = jnp.sum(grad_parts.astype(jnp.float32), axis=0).astype(jnp.bfloat16)
    out_inverse = inverse_order(pattern[0])
    in_inverse = inverse_order(pattern[1])
    numbers = jnp.arange(NB * NB, dtype=jnp.int32)

    def single(item_pair):
        number, gradient = item_pair
        out_place = out_inverse[number // NB]
        in_place = in_inverse[number % NB]
        return precondition(gradient, bases_used[0, out_place], bases_used[1, in_place],
                            eigenvalues[0, out_place], eigenvalues[1, in_place])

    precond = lax.map(single, (numbers, summed))
    return precond, eigenvalues.reshape(2 * NB, BS)
```

```python
import jax
import jax.numpy as jnp
from jax import lax
from jax.experimental import pallas as pl
from jax.experimental.pallas import tpu as pltpu
from jax.sharding import PartitionSpec as P

DAMPING = 0.5
NB = 8
BS = 512
RING = 4
PIECE = BS // RING
ROWS = PIECE // RING
TILE = 512
MESH = pl.DeviceIdType.MESH
N_SEMS = 128


def kernel(token_count, pattern, owners, tokens, outgrads, grads, slot, precond, eigen_out,
           values, bases, picked, own_grads, grad_in, part_out, part_in, summed, rotated,
           eig, eig_x, eig_y, eig_z, both, send_sems, recv_sems, local_sems):
    dp, mp = lax.axis_index("dp"), lax.axis_index("mp")
    y, z_hi = dp // 2, dp % 2
    core, x, z_lo = mp % 2, (mp // 2) % RING, mp // (2 * RING)
    z = z_hi * RING + z_lo
    side_row = z_lo * (1 - core) + x * core
    side_col = x * (1 - core) + z_lo * core

    def device(dx=0, dy=0, dz=0, dc=0):
        tx, ty, tz = (x + dx + 8) % 4, (y + dy + 8) % 4, (z + dz + 16) % 8
        tc = (core + dc) % 2
        return (ty * 2 + tz // 4, ((tz % 4) * 4 + tx) * 2 + tc)

    def along_row(d):
        return device(dx=d * core, dz=d * (1 - core))

    def along_col(d):
        return device(dx=d * (1 - core), dz=d * core)

    sibling = device(dc=1)
    count = [0]
    pending = []

    def remote(src, dst, target, again=False):
        if not again:
            count[0] += 1
        n = count[0]
        return pltpu.make_async_remote_copy(
            src_ref=src, dst_ref=dst, send_sem=send_sems.at[n], recv_sem=recv_sems.at[n],
            device_id=target, device_id_type=MESH)

    def go(copy):
        copy.start()
        pending.append(copy)
        return copy

    def flush():
        for copy in pending:
            copy.wait_send()
        pending.clear()

    far = 2 - 4 * core
    plane = [(dx, dz) for dz in (1, -1, 0, None) for dx in (1, 3, 0, 2) if dx or dz != 0]
    offsets = [dict(dx=dx, dz=far if dz is None else dz) for dx, dz in plane]
    offsets += [dict(dz=-far), dict(dz=3), dict(dz=-3), dict(dz=4)]
    offsets += [dict(dy=1), dict(dy=3), dict(dy=2)]
    offsets += [dict(dc=1)]

    locals_ = []

    def local(n, src, dst):
        copy = pltpu.make_async_copy(src, dst, local_sems.at[n])
        copy.start()
        return copy

    tokens_here = tokens.shape[0]
    mine = values.at[pl.ds(0, tokens_here)]
    theirs = values.at[pl.ds(tokens_here, tokens_here)]
    chip = z_lo * RING + x

    def piece(row, col):
        return slot.at[pl.ds(pl.multiple_of(row * PIECE + y * ROWS, ROWS), ROWS),
                       pl.ds(pl.multiple_of(col * PIECE, PIECE), PIECE)]

    own_a = local(0, piece(side_row, side_col), picked.at[0, chip])
    own_b = local(1, piece(side_col, side_row), picked.at[2, chip])
    own_g = local(2, grads.at[0, :, pl.ds(pl.multiple_of(y * PIECE, PIECE), PIECE)], own_grads)

    @pl.when(core == 0)
    def _():
        pltpu.make_async_copy(outgrads, mine, local_sems.at[3]).start()

    @pl.when(core == 1)
    def _():
        pltpu.make_async_copy(tokens, mine, local_sems.at[3]).start()

    barrier = pltpu.get_barrier_semaphore()
    for off in offsets:
        back = {k: -v for k, v in off.items()}
        pl.semaphore_signal(barrier, inc=1, device_id=device(**back), device_id_type=MESH)
    pl.semaphore_wait(barrier, len(offsets))

    scatter = []
    for dx, dz in plane:
        dz = far if dz is None else dz
        tx, tz = (x + dx) % 4, (z + dz + 16) % 4
        row = tz * (1 - core) + tx * core
        col = tx * (1 - core) + tz * core
        target = device(dx=dx, dz=dz)
        scatter.append(go(remote(piece(row, col), picked.at[0, chip], target)))
        scatter.append(go(remote(piece(col, row), picked.at[2, chip], target)))

    cross_values = remote(tokens, theirs, sibling)
    cross_outgrads = remote(outgrads, theirs, sibling, again=True)

    @pl.when(core == 0)
    def _():
        cross_values.start()

    @pl.when(core == 1)
    def _():
        cross_outgrads.start()

    pending.append(cross_values)

    def send_quarters(block):
        sent = []
        for j, dy in enumerate((1, 3, 2)):
            ty = (y + dy) % 4
            src = grads.at[0, block, pl.ds(pl.multiple_of(ty * PIECE, PIECE), PIECE)]
            sent.append(go(remote(src, grad_in.at[j, block], device(dy=dy))))
        return sent

    quarters = [send_quarters(0)]

    own_a.wait()
    own_b.wait()
    for copy in scatter:
        copy.wait_recv()
    to_sibling = go(remote(picked.at[2], picked.at[1], sibling))
    wanted = []
    for p in range(NB):
        owner = jnp.int32(0)
        for b in range(NB):
            owner += jnp.where(pattern[core, b] == p, owners[core * NB + b], 0)
        wanted.append(jnp.where(owner % 2 == core, 0, 16) + owner // 2)
    to_sibling.wait_recv()
    first_row = pl.multiple_of(side_row * PIECE + y * ROWS, ROWS)
    for p in range(NB):
        index = wanted[p]
        bases[p, side_col, pl.ds(first_row, ROWS), :] = picked[index // 16, index % 16]

    fine = bases.at[pl.ds(0, NB), side_col, pl.ds(first_row, ROWS)]
    fines = [go(remote(fine, fine, device(dy=dy))) for dy in (1, 3, 2)]
    quarters.append(send_quarters(1))
    for copy in fines:
        copy.wait_recv()

    def chunk(row, half=None):
        rows = pl.ds(pl.multiple_of(((side_row + row + 4) % 4) * PIECE, PIECE), PIECE)
        some = pl.ds(0, NB) if half is None else pl.ds(half * (NB // 2), NB // 2)
        return some, rows

    def at(row, col, half=None):
        some, rows = chunk(row, half)
        return bases.at[some, (side_col + col + 4) % 4, rows]

    def send(ref, target):
        return go(remote(ref, ref, target))

    rows_up = send(at(0, 0), along_row(1))
    rows_down = send(at(0, 0), along_row(-1))
    arriving = {}
    for row in (0,):
        arriving[row] = (send(at(row, 0), along_col(1)), send(at(row, 0), along_col(-1)))
    rows_up.wait_recv()
    rows_up_far = send(at(-1, 0, 0), along_row(1))
    rows_down.wait_recv()
    rows_down_far = send(at(1, 0, 1), along_row(-1))
    for row in (-1, 1):
        arriving[row] = (send(at(row, 0), along_col(1)), send(at(row, 0), along_col(-1)))

    z_parts = []
    for block in range(2):
        if block == 0:
            own_g.wait()
        for copy in quarters[block]:
            copy.wait_recv()
        total = own_grads[block].astype(jnp.float32)
        for j in range(3):
            total += grad_in[j, block].astype(jnp.float32)
        part_out[block] = total.astype(jnp.bfloat16)
        z_parts.append(go(remote(part_out.at[block], part_in.at[block], device(dz=4))))

    far_halves = {}

    def pass_on(row):
        up, down = arriving[row]
        up.wait_recv()
        first = send(at(row, -1, 0), along_col(1))
        down.wait_recv()
        second = send(at(row, 1, 1), along_col(-1))
        far_halves[row] = (first, second)

    pass_on(0)
    rows_up_far.wait_recv()
    rows_down_far.wait_recv()
    arriving[2] = (send(at(2, 0), along_col(1)), send(at(2, 0), along_col(-1)))

    own_values = pltpu.make_async_copy(tokens, mine, local_sems.at[3])
    own_values.wait()
    cross_values.wait_recv()

    def project(col):
        place = (side_col + col + 4) % 4
        columns = pl.ds(pl.multiple_of(place * PIECE, PIECE), PIECE)

        def one(p, sums):
            weights = bases[p, place]

            def tile(t, total):
                block = values[pl.ds(pl.multiple_of(t * TILE, TILE), TILE),
                               pl.ds(pl.multiple_of(p * BS, BS), BS)]
                out = jnp.dot(block, weights, preferred_element_type=jnp.float32)
                return total + jnp.sum((out * out).reshape(TILE // 8, 8, PIECE), axis=0)

            total = lax.fori_loop(0, 2 * tokens_here // TILE, tile, jnp.zeros((8, PIECE), jnp.float32))
            here = lax.broadcasted_iota(jnp.int32, (NB, PIECE), 0) == p
            return jnp.where(here, jnp.sum(total, axis=0, keepdims=True), sums)

        eig[:, columns] = lax.fori_loop(0, NB, one, jnp.zeros((NB, PIECE), jnp.float32))

    project(0)
    for row in (-1, 1, 2):
        pass_on(row)
    project(-1)
    project(1)

    own_rows = pl.ds(pl.multiple_of(y * PIECE, PIECE), PIECE)
    whole = []
    for block in range(2):
        z_parts[block].wait_recv()
        total = part_out[block].astype(jnp.float32) + part_in[block].astype(jnp.float32)
        summed[block, own_rows] = total.astype(jnp.bfloat16)
        ref = summed.at[block, own_rows]
        whole += [go(remote(ref, ref, device(dy=dy))) for dy in (1, 3, 2)]

    for row in (0, -1, 1, 2):
        for copy in far_halves[row]:
            copy.wait_recv()
    project(2)

    eig_x[x] = eig[...]
    over_x = [go(remote(eig, eig_x.at[x], device(dx=dx))) for dx in (1, 3, 2)]

    out_place = z_lo * 2 + x // 2
    in_place = (x % 2) * 4
    one_basis = remote(bases.at[out_place], bases.at[NB], sibling)
    two_bases = remote(bases.at[pl.ds(in_place, 2)], bases.at[pl.ds(NB, 2)], sibling)

    @pl.when(core == 0)
    def _():
        one_basis.start()

    @pl.when(core == 1)
    def _():
        two_bases.start()

    for copy in over_x:
        copy.wait_recv()
    eig_y[y] = (eig_x[0] + eig_x[1]) + (eig_x[2] + eig_x[3])
    over_y = [go(remote(eig_y.at[y], eig_y.at[y], device(dy=dy))) for dy in (1, 3, 2)]

    @pl.when(core == 0)
    def _():
        two_bases.wait_recv()
        one_basis.wait_send()

    @pl.when(core == 1)
    def _():
        one_basis.wait_recv()
        two_bases.wait_send()

    for copy in over_y:
        copy.wait_recv()
    eig_z[z] = (eig_y[0] + eig_y[1]) + (eig_y[2] + eig_y[3])
    over_z = [go(remote(eig_z.at[z], eig_z.at[z], device(dz=dz))) for dz in (1, -1, 2, -2, 3, -3, 4)]

    out_basis = out_place * (1 - core) + NB * core

    def in_basis(j):
        return (NB + j) * (1 - core) + (in_place + 2 + j) * core

    def basis(place):
        return jnp.concatenate([bases[place, col] for col in range(RING)], axis=1)

    for copy in whole:
        copy.wait_recv()

    def rotate(j, _):
        halfway = lax.dot_general(basis(out_basis), summed[j], (((0,), (0,)), ((), ())),
                                  preferred_element_type=jnp.float32).astype(jnp.bfloat16)
        rotated[j] = jnp.dot(halfway, basis(in_basis(j)), preferred_element_type=jnp.float32)
        return 0

    lax.fori_loop(0, 2, rotate, 0)
    flush_later = list(pending)
    pending.clear()
    for copy in over_z:
        copy.wait_recv()
    total = (eig_z[0] + eig_z[1]) + (eig_z[2] + eig_z[3])
    total += (eig_z[4] + eig_z[5]) + (eig_z[6] + eig_z[7])
    both[core] = total / token_count
    across = go(remote(both.at[core], both.at[core], sibling))
    across.wait_recv()

    for s in range(2):
        for b in range(NB):
            eigen_out[s * NB + b: s * NB + b + 1, :] = both[s, pl.ds(pattern[s, b], 1), :]

    out_scale = both[0, pl.ds(out_place, 1), :].reshape(BS, 1)

    def finish(j, _):
        in_scale = both[1, pl.ds(in_place + 2 * core + j, 1), :]
        scaled = (rotated[j] / (out_scale * in_scale + DAMPING)).astype(jnp.bfloat16)
        returned = jnp.dot(basis(out_basis), scaled, preferred_element_type=jnp.float32).astype(jnp.bfloat16)
        precond[j] = lax.dot_general(returned, basis(in_basis(j)), (((1,), (1,)), ((), ())),
                                     preferred_element_type=jnp.float32).astype(jnp.bfloat16)
        return 0

    lax.fori_loop(0, 2, finish, 0)
    flush()
    for copy in flush_later:
        copy.wait_send()


def local(token_total, tokens, outgrads, grad_parts, basis_slots, pattern, owners):
    here = tokens.shape[0]
    bf16, f32 = jnp.bfloat16, jnp.float32
    anywhere = pl.BlockSpec(memory_space=pl.ANY)
    scalars = pl.BlockSpec(memory_space=pltpu.SMEM)
    vmem = pl.BlockSpec(memory_space=pltpu.VMEM)

    def body(*refs):
        kernel(float(token_total), *refs)

    return pl.pallas_call(
        body,
        out_shape=(jax.ShapeDtypeStruct((2, BS, BS), bf16), jax.ShapeDtypeStruct((2 * NB, BS), f32)),
        in_specs=[scalars, scalars, anywhere, anywhere, anywhere, anywhere],
        out_specs=(vmem, vmem),
        scratch_shapes=[
            pltpu.VMEM((2 * here, NB * BS), bf16),
            pltpu.VMEM((NB + 2, RING, BS, PIECE), bf16),
            pltpu.VMEM((3, 16, ROWS, PIECE), bf16),
            pltpu.VMEM((2, PIECE, BS), bf16),
            pltpu.VMEM((3, 2, PIECE, BS), bf16),
            pltpu.VMEM((2, PIECE, BS), bf16),
            pltpu.VMEM((2, PIECE, BS), bf16),
            pltpu.VMEM((2, BS, BS), bf16),
            pltpu.VMEM((2, BS, BS), f32),
            pltpu.VMEM((NB, BS), f32),
            pltpu.VMEM((4, NB, BS), f32),
            pltpu.VMEM((4, NB, BS), f32),
            pltpu.VMEM((8, NB, BS), f32),
            pltpu.VMEM((2, NB, BS), f32),
            pltpu.SemaphoreType.DMA((N_SEMS,)),
            pltpu.SemaphoreType.DMA((N_SEMS,)),
            pltpu.SemaphoreType.DMA((4,)),
        ],
        compiler_params=pltpu.CompilerParams(
            collective_id=0, has_side_effects=True, vmem_limit_bytes=48 * 2 ** 20),
    )(pattern, owners, tokens, outgrads, grad_parts, basis_slots.reshape(BS, BS))


def solution(mesh):
    placed = (
        P(("dp", "mp"), None),
        P(("dp", "mp"), None),
        P("dp", "mp", None, None),
        P("mp", None, None),
        P(),
        P(),
    )

    def whole(tokens, *rest):
        total = tokens.shape[0]
        return jax.shard_map(
            lambda *args: local(total, *args), mesh=mesh, in_specs=placed,
            out_specs=(P("mp", None, None), P()), check_vma=False)(tokens, *rest)

    return whole
```

```python
import jax
import jax.numpy as jnp
from jax import lax
from jax.experimental import pallas as pl
from jax.experimental.pallas import tpu as pltpu
from jax.sharding import PartitionSpec as P

DAMPING = 0.5
NB = 8
BS = 512
RING = 4
PIECE = BS // RING
ROWS = PIECE // RING
MESH = pl.DeviceIdType.MESH
N_SEMS = 128


class Far:
    def __init__(self, sign):
        self.sign = sign

    def __neg__(self):
        return Far(-self.sign)


def kernel(token_count, pattern_in, owners_in, tokens, outgrads, grads, slot, precond, eigen_out,
           pattern, owners, values, bases, picked, own_grads, grad_in, part_out, part_in, summed, rotated,
           eig, eig_x, eig_y, eig_z, both, send_sems, recv_sems, local_sems):
    dp, mp = lax.axis_index("dp"), lax.axis_index("mp")
    y, z_hi = lax.div(dp, 2), lax.rem(dp, 2)
    core, chip = lax.rem(mp, 2), lax.div(mp, 2)
    x, z_lo = lax.rem(chip, RING), lax.div(chip, RING)
    z = z_hi * RING + z_lo
    known = {}

    def wrapped(name, value, delta, size):
        if (name, delta) not in known:
            known[name, delta] = lax.rem(value + (delta + size), size) if delta else value
        return known[name, delta]

    def mp_part(dx, dz):
        if ("mp", dx, dz) not in known:
            known["mp", dx, dz] = wrapped("z_lo", z_lo, dz % 4, 4) * 8 + wrapped("x", x, dx % 4, 4) * 2
        return known["mp", dx, dz]

    def dp_part(dy, dz):
        if ("dp", dy, dz) not in known:
            known["dp", dy, dz] = wrapped("y", y, dy % 4, 4) * 2 + lax.div(wrapped("z", z, dz % 8, 8), 4)
        return known["dp", dy, dz]
    side_row = z_lo * (1 - core) + x * core
    side_col = x * (1 - core) + z_lo * core

    def device(dx=0, dy=0, dz=0, dc=0):
        if isinstance(dz, Far):
            first, second = device(dx, dy, 2 * dz.sign, dc), device(dx, dy, -2 * dz.sign, dc)
            return tuple(a + (b - a) * core for a, b in zip(first, second))
        return (dp_part(dy, dz), mp_part(dx, dz) + (core if dc == 0 else 1 - core))

    def along(d):
        if ("along", d) not in known:
            over_x, over_z = device(dx=d), device(dz=d)
            known["along", d] = (
                tuple(b + (a - b) * core for a, b in zip(over_x, over_z)),
                tuple(a + (b - a) * core for a, b in zip(over_x, over_z)))
        return known["along", d]

    def along_row(d):
        return along(d)[0]

    def along_col(d):
        return along(d)[1]

    sibling = device(dc=1)
    count = [0]
    pending = []

    def remote(src, dst, target, again=False):
        if not again:
            count[0] += 1
        n = count[0]
        return pltpu.make_async_remote_copy(
            src_ref=src, dst_ref=dst, send_sem=send_sems.at[n], recv_sem=recv_sems.at[n],
            device_id=target, device_id_type=MESH)

    def go(copy):
        copy.start()
        pending.append(copy)
        return copy

    def flush():
        for copy in pending:
            copy.wait_send()
        pending.clear()

    far = Far(1)
    plane = [(dx, dz) for dz in (1, -1, 0, far) for dx in (1, 3, 0, 2) if dx or dz != 0]
    offsets = [dict(dx=dx, dz=dz) for dx, dz in plane]
    offsets += [dict(dz=-far), dict(dz=3), dict(dz=-3), dict(dz=4)]
    offsets += [dict(dy=1), dict(dy=3), dict(dy=2)]
    offsets += [dict(dc=1)]

    def local(n, src, dst):
        copy = pltpu.make_async_copy(src, dst, local_sems.at[n])
        copy.start()
        return copy

    tokens_here = tokens.shape[0]
    mine = values.at[pl.ds(0, tokens_here)]
    theirs = values.at[pl.ds(tokens_here, tokens_here)]
    def piece(row, col):
        return slot.at[pl.ds(pl.multiple_of(row * PIECE + y * ROWS, ROWS), ROWS),
                       pl.ds(pl.multiple_of(col * PIECE, PIECE), PIECE)]

    own_p = local(4, pattern_in, pattern)
    own_o = local(5, owners_in, owners)
    own_a = local(0, piece(side_row, side_col), picked.at[0, chip])
    own_b = local(1, piece(side_col, side_row), picked.at[2, chip])
    own_g = local(2, grads.at[0, :, pl.ds(pl.multiple_of(y * PIECE, PIECE), PIECE)], own_grads)

    @pl.when(core == 0)
    def _():
        pltpu.make_async_copy(outgrads, mine, local_sems.at[3]).start()

    @pl.when(core == 1)
    def _():
        pltpu.make_async_copy(tokens, mine, local_sems.at[3]).start()

    barrier = pltpu.get_barrier_semaphore()
    for off in offsets:
        back = {k: -v for k, v in off.items()}
        pl.semaphore_signal(barrier, inc=1, device_id=device(**back), device_id_type=MESH)
    pl.semaphore_wait(barrier, len(offsets))

    scatter = []
    for dx, dz in plane:
        tx = wrapped("x", x, dx, 4)
        tz = wrapped("z_lo", z_lo, 2 if dz is far else dz % 4, 4)
        row = tz * (1 - core) + tx * core
        col = tx * (1 - core) + tz * core
        target = device(dx=dx, dz=dz)
        scatter.append(go(remote(piece(row, col), picked.at[0, chip], target)))
        scatter.append(go(remote(piece(col, row), picked.at[2, chip], target)))

    def send_quarters(block):
        sent = []
        for j, dy in enumerate((1, 3, 2)):
            ty = wrapped("y", y, dy, 4)
            src = grads.at[0, block, pl.ds(pl.multiple_of(ty * PIECE, PIECE), PIECE)]
            sent.append(go(remote(src, grad_in.at[j, block], device(dy=dy))))
        return sent

    quarters = [send_quarters(0)]

    for copy in (own_p, own_o, own_a, own_b):
        copy.wait()
    for copy in scatter:
        copy.wait_recv()
    to_sibling = go(remote(picked.at[2], picked.at[1], sibling))
    wanted = []
    for p in range(NB):
        owner = jnp.int32(0)
        for b in range(NB):
            owner += jnp.where(pattern[core, b] == p, owners[core * NB + b], 0)
        wanted.append((jnp.where(lax.rem(owner, 2) == core, 0, 1), lax.div(owner, 2)))
    to_sibling.wait_recv()
    for p in range(NB):
        bases[p, side_col, side_row, 0] = picked[wanted[p]]

    def unit(row, col, quarters, half=None):
        some = pl.ds(0, NB) if half is None else pl.ds(half * (NB // 2), NB // 2)
        place = wrapped("col", side_col, col % 4, 4), wrapped("row", side_row, row % 4, 4)
        return bases.at[some, place[0], place[1], pl.ds(*quarters)]

    def send(ref, target):
        return go(remote(ref, ref, target))

    own, rest = (0, 1), (1, 3)
    over_rows, over_cols, far_cols = {}, {}, {}

    def both_ways(row, part):
        over_cols[row, part] = (send(unit(row, 0, part), along_col(1)), send(unit(row, 0, part), along_col(-1)))

    def have_own(row):
        over_rows[row] = [
            go(remote(unit(row, 0, own), unit(row, 0, (4 - dy, 1)), device(dy=dy))) for dy in (1, 3, 2)]
        both_ways(row, own)

    def have_rest(row):
        for copy in over_rows[row]:
            copy.wait_recv()
        both_ways(row, rest)

    def pass_on(row, part):
        up, down = over_cols[row, part]
        up.wait_recv()
        first = send(unit(row, -1, part, 0), along_col(1))
        down.wait_recv()
        second = send(unit(row, 1, part, 1), along_col(-1))
        far_cols[row, part] = (first, second)

    rows_up = send(unit(0, 0, own), along_row(1))
    rows_down = send(unit(0, 0, own), along_row(-1))
    have_own(0)
    cross_values = remote(tokens, theirs, sibling)
    cross_outgrads = remote(outgrads, theirs, sibling, again=True)

    @pl.when(core == 0)
    def _():
        cross_values.start()

    @pl.when(core == 1)
    def _():
        cross_outgrads.start()

    pending.append(cross_values)

    z_parts = []

    def partial_sum(block):
        if block == 0:
            own_g.wait()
        for copy in quarters[block]:
            copy.wait_recv()
        total = own_grads[block].astype(jnp.float32)
        for j in range(3):
            total += grad_in[j, block].astype(jnp.float32)
        part_out[block] = total.astype(jnp.bfloat16)
        z_parts.append(go(remote(part_out.at[block], part_in.at[block], device(dz=4))))

    rows_up.wait_recv()
    rows_up_far = send(unit(-1, 0, own, 0), along_row(1))
    rows_down.wait_recv()
    rows_down_far = send(unit(1, 0, own, 1), along_row(-1))
    have_own(-1)
    have_own(1)
    pass_on(0, own)
    have_rest(0)
    rows_up_far.wait_recv()
    rows_down_far.wait_recv()
    have_own(2)
    quarters.append(send_quarters(1))
    pass_on(-1, own)
    pass_on(1, own)
    partial_sum(0)
    have_rest(-1)
    pass_on(0, rest)
    have_rest(1)
    pass_on(2, own)
    have_rest(2)

    own_values = pltpu.make_async_copy(tokens, mine, local_sems.at[3])
    own_values.wait()
    cross_values.wait_recv()

    turned = [lax.rem(k + 4 - y, 4) for k in range(4)]

    def columns_of(p, place):
        return jnp.concatenate([bases[p, place, row, turn] for row in range(RING) for turn in turned], axis=0)

    def project(*cols):
        places = [wrapped("col", side_col, col % 4, 4) for col in cols]
        width = PIECE * len(cols)

        def one(p, sums):
            weights = jnp.concatenate([columns_of(p, place) for place in places], axis=1)
            block = values[:, pl.ds(pl.multiple_of(p * BS, BS), BS)]
            out = jnp.dot(block, weights, preferred_element_type=jnp.float32)
            total = jnp.sum((out * out).reshape(2 * tokens_here // 8, 8, width), axis=0)
            here = lax.broadcasted_iota(jnp.int32, (NB, width), 0) == p
            return jnp.where(here, jnp.sum(total, axis=0, keepdims=True), sums)

        sums = lax.fori_loop(0, NB, one, jnp.zeros((NB, width), jnp.float32), unroll=4)
        for n, place in enumerate(places):
            columns = pl.ds(pl.multiple_of(place * PIECE, PIECE), PIECE)
            eig[:, columns] = sums[:, n * PIECE:(n + 1) * PIECE]

    pass_on(-1, rest)
    project(0)
    pass_on(1, rest)
    pass_on(2, rest)
    project(-1, 1)
    partial_sum(1)

    for copies in far_cols.values():
        for copy in copies:
            copy.wait_recv()
    project(2)

    eig_x[x] = eig[...]
    over_x = [go(remote(eig, eig_x.at[x], device(dx=dx))) for dx in (1, 3, 2)]

    own_rows = pl.ds(pl.multiple_of(y * PIECE, PIECE), PIECE)
    whole = []
    for block in range(2):
        z_parts[block].wait_recv()
        total = part_out[block].astype(jnp.float32) + part_in[block].astype(jnp.float32)
        summed[block, own_rows] = total.astype(jnp.bfloat16)
        ref = summed.at[block, own_rows]
        whole += [go(remote(ref, ref, device(dy=dy))) for dy in (1, 3, 2)]

    out_place = z_lo * 2 + lax.div(x, 2)
    in_place = lax.rem(x, 2) * 4
    one_basis = remote(bases.at[out_place], bases.at[NB], sibling)
    two_bases = remote(bases.at[pl.ds(in_place, 2)], bases.at[pl.ds(NB, 2)], sibling)

    @pl.when(core == 0)
    def _():
        one_basis.start()

    @pl.when(core == 1)
    def _():
        two_bases.start()

    for copy in over_x:
        copy.wait_recv()
    eig_y[y] = (eig_x[0] + eig_x[1]) + (eig_x[2] + eig_x[3])
    over_y = [go(remote(eig_y.at[y], eig_y.at[y], device(dy=dy))) for dy in (1, 3, 2)]

    @pl.when(core == 0)
    def _():
        two_bases.wait_recv()
        one_basis.wait_send()

    @pl.when(core == 1)
    def _():
        one_basis.wait_recv()
        two_bases.wait_send()

    for copy in over_y:
        copy.wait_recv()
    eig_z[z] = (eig_y[0] + eig_y[1]) + (eig_y[2] + eig_y[3])
    over_z = [go(remote(eig_z.at[z], eig_z.at[z], device(dz=dz))) for dz in (1, -1, 2, -2, 3, -3, 4)]

    out_basis = out_place * (1 - core) + NB * core

    def in_basis(j):
        return (NB + j) * (1 - core) + (in_place + 2 + j) * core

    def basis(place):
        return jnp.concatenate([columns_of(place, col) for col in range(RING)], axis=1)

    for copy in whole:
        copy.wait_recv()

    def rotate(j, _):
        halfway = lax.dot_general(basis(out_basis), summed[j], (((0,), (0,)), ((), ())),
                                  preferred_element_type=jnp.float32).astype(jnp.bfloat16)
        rotated[j] = jnp.dot(halfway, basis(in_basis(j)), preferred_element_type=jnp.float32)
        return 0

    lax.fori_loop(0, 2, rotate, 0)
    flush_later = list(pending)
    pending.clear()
    for copy in over_z:
        copy.wait_recv()
    total = (eig_z[0] + eig_z[1]) + (eig_z[2] + eig_z[3])
    total += (eig_z[4] + eig_z[5]) + (eig_z[6] + eig_z[7])
    both[core] = total / token_count
    across = go(remote(both.at[core], both.at[core], sibling))
    across.wait_recv()

    for s in range(2):
        for b in range(NB):
            eigen_out[s * NB + b: s * NB + b + 1, :] = both[s, pl.ds(pattern[s, b], 1), :]

    out_scale = both[0, pl.ds(out_place, 1), :].reshape(BS, 1)

    def finish(j, _):
        in_scale = both[1, pl.ds(in_place + 2 * core + j, 1), :]
        scaled = (rotated[j] / (out_scale * in_scale + DAMPING)).astype(jnp.bfloat16)
        returned = jnp.dot(basis(out_basis), scaled, preferred_element_type=jnp.float32).astype(jnp.bfloat16)
        precond[j] = lax.dot_general(returned, basis(in_basis(j)), (((1,), (1,)), ((), ())),
                                     preferred_element_type=jnp.float32).astype(jnp.bfloat16)
        return 0

    lax.fori_loop(0, 2, finish, 0)
    flush()
    for copy in flush_later:
        copy.wait_send()


def local(token_total, tokens, outgrads, grad_parts, basis_slots, pattern, owners):
    here = tokens.shape[0]
    bf16, f32 = jnp.bfloat16, jnp.float32
    anywhere = pl.BlockSpec(memory_space=pl.ANY)
    vmem = pl.BlockSpec(memory_space=pltpu.VMEM)

    def body(*refs):
        kernel(float(token_total), *refs)

    operands = (pattern, owners, tokens, outgrads, grad_parts, basis_slots.reshape(BS, BS))
    return pl.pallas_call(
        body,
        out_shape=(jax.ShapeDtypeStruct((2, BS, BS), bf16), jax.ShapeDtypeStruct((2 * NB, BS), f32)),
        in_specs=[anywhere] * 6,
        out_specs=(vmem, vmem),
        scratch_shapes=[
            pltpu.SMEM((2, NB), jnp.int32),
            pltpu.SMEM((2 * NB,), jnp.int32),
            pltpu.VMEM((2 * here, NB * BS), bf16),
            pltpu.VMEM((NB + 2, RING, RING, RING, ROWS, PIECE), bf16),
            pltpu.VMEM((3, 16, ROWS, PIECE), bf16),
            pltpu.VMEM((2, PIECE, BS), bf16),
            pltpu.VMEM((3, 2, PIECE, BS), bf16),
            pltpu.VMEM((2, PIECE, BS), bf16),
            pltpu.VMEM((2, PIECE, BS), bf16),
            pltpu.VMEM((2, BS, BS), bf16),
            pltpu.VMEM((2, BS, BS), f32),
            pltpu.VMEM((NB, BS), f32),
            pltpu.VMEM((4, NB, BS), f32),
            pltpu.VMEM((4, NB, BS), f32),
            pltpu.VMEM((8, NB, BS), f32),
            pltpu.VMEM((2, NB, BS), f32),
            pltpu.SemaphoreType.DMA((N_SEMS,)),
            pltpu.SemaphoreType.DMA((N_SEMS,)),
            pltpu.SemaphoreType.DMA((6,)),
        ],
        compiler_params=pltpu.CompilerParams(
            collective_id=0, has_side_effects=True, vmem_limit_bytes=48 * 2 ** 20),
    )(*[pltpu.with_memory_space_constraint(operand, pltpu.HBM) for operand in operands])


def solution(mesh):
    placed = (
        P(("dp", "mp"), None),
        P(("dp", "mp"), None),
        P("dp", "mp", None, None),
        P("mp", None, None),
        P(),
        P(),
    )

    def whole(tokens, *rest):
        total = tokens.shape[0]
        return jax.shard_map(
            lambda *args: local(total, *args), mesh=mesh, in_specs=placed,
            out_specs=(P("mp", None, None), P()), check_vma=False)(tokens, *rest)

    return whole
```

```python
import jax
import jax.numpy as jnp
from jax import lax
from jax.experimental import pallas as pl
from jax.experimental.pallas import tpu as pltpu
from jax.sharding import PartitionSpec as P

DAMPING = 0.5
NB = 8
BS = 512
RING = 4
PIECE = BS // RING
ROWS = PIECE // RING
MESH = pl.DeviceIdType.MESH
N_SEMS = 128


class Far:
    def __init__(self, sign):
        self.sign = sign

    def __neg__(self):
        return Far(-self.sign)


def kernel(token_count, pattern_in, owners_in, tokens, outgrads, grads, slot, precond, eigen_out,
           pattern, owners, slot_quarter, values, bases, picked, own_grads, grad_in, part_out, part_in, summed, rotated,
           eig, eig_x, eig_y, eig_z, both, send_sems, recv_sems, local_sems):
    dp, mp = lax.axis_index("dp"), lax.axis_index("mp")
    y, z_hi = lax.div(dp, 2), lax.rem(dp, 2)
    core, chip = lax.rem(mp, 2), lax.div(mp, 2)
    x, z_lo = lax.rem(chip, RING), lax.div(chip, RING)
    z = z_hi * RING + z_lo
    known = {}

    def wrapped(name, value, delta, size):
        if (name, delta) not in known:
            known[name, delta] = lax.rem(value + (delta + size), size) if delta else value
        return known[name, delta]

    def mp_part(dx, dz):
        if ("mp", dx, dz) not in known:
            known["mp", dx, dz] = wrapped("z_lo", z_lo, dz % 4, 4) * 8 + wrapped("x", x, dx % 4, 4) * 2
        return known["mp", dx, dz]

    def dp_part(dy, dz):
        if ("dp", dy, dz) not in known:
            known["dp", dy, dz] = wrapped("y", y, dy % 4, 4) * 2 + lax.div(wrapped("z", z, dz % 8, 8), 4)
        return known["dp", dy, dz]
    side_row = z_lo * (1 - core) + x * core
    side_col = x * (1 - core) + z_lo * core

    def device(dx=0, dy=0, dz=0, dc=0):
        if isinstance(dz, Far):
            first, second = device(dx, dy, 2 * dz.sign, dc), device(dx, dy, -2 * dz.sign, dc)
            return tuple(a + (b - a) * core for a, b in zip(first, second))
        return (dp_part(dy, dz), mp_part(dx, dz) + (core if dc == 0 else 1 - core))

    def along(d):
        if ("along", d) not in known:
            over_x, over_z = device(dx=d), device(dz=d)
            known["along", d] = (
                tuple(b + (a - b) * core for a, b in zip(over_x, over_z)),
                tuple(a + (b - a) * core for a, b in zip(over_x, over_z)))
        return known["along", d]

    def along_row(d):
        return along(d)[0]

    def along_col(d):
        return along(d)[1]

    sibling = device(dc=1)
    count = [0]
    pending = []

    def remote(src, dst, target, again=False):
        if not again:
            count[0] += 1
        n = count[0]
        return pltpu.make_async_remote_copy(
            src_ref=src, dst_ref=dst, send_sem=send_sems.at[n], recv_sem=recv_sems.at[n],
            device_id=target, device_id_type=MESH)

    def go(copy):
        copy.start()
        pending.append(copy)
        return copy

    def flush():
        for copy in pending:
            copy.wait_send()
        pending.clear()

    far = Far(1)
    plane = [(dx, dz) for dz in (far, 1, -1, 0) for dx in (2, 1, 3, 0) if dx or dz != 0]
    hops = {0: 0, 1: 1, -1: 1, 2: 2, 3: 1, far: 2}
    plane.sort(key=lambda step: -hops[step[0]] - hops[step[1]])
    offsets = [dict(dx=dx, dz=dz) for dx, dz in plane]
    offsets += [dict(dz=-far), dict(dz=3), dict(dz=-3), dict(dz=4)]
    offsets += [dict(dy=1), dict(dy=3), dict(dy=2)]
    offsets += [dict(dc=1)]

    def local(n, src, dst):
        copy = pltpu.make_async_copy(src, dst, local_sems.at[n])
        copy.start()
        return copy

    tokens_here = tokens.shape[0]
    mine = values.at[pl.ds(0, tokens_here)]
    theirs = values.at[pl.ds(tokens_here, tokens_here)]

    def piece(row, col):
        return slot_quarter.at[row, :, pl.ds(pl.multiple_of(col * PIECE, PIECE), PIECE)]

    barrier = pltpu.get_barrier_semaphore()
    for off in offsets:
        back = {k: -v for k, v in off.items()}
        pl.semaphore_signal(barrier, inc=1, device_id=device(**back), device_id_type=MESH)
    own_p = local(4, pattern_in, pattern)
    own_o = local(5, owners_in, owners)
    own_s = local(6, slot.at[:, pl.ds(pl.multiple_of(y * ROWS, ROWS), ROWS)], slot_quarter)
    own_g = local(2, grads.at[0, :, pl.ds(pl.multiple_of(y * PIECE, PIECE), PIECE)], own_grads)

    @pl.when(core == 0)
    def _():
        pltpu.make_async_copy(outgrads, mine, local_sems.at[3]).start()

    @pl.when(core == 1)
    def _():
        pltpu.make_async_copy(tokens, mine, local_sems.at[3]).start()

    pl.semaphore_wait(barrier, len(offsets))

    def send_quarters(block):
        sent = []
        for j, dy in enumerate((1, 3, 2)):
            ty = wrapped("y", y, dy, 4)
            src = grads.at[0, block, pl.ds(pl.multiple_of(ty * PIECE, PIECE), PIECE)]
            sent.append(go(remote(src, grad_in.at[j, block], device(dy=dy))))
        return sent

    quarters = [send_quarters(0)]

    own_s.wait()
    own_a = local(0, piece(side_row, side_col), picked.at[0, chip])
    own_b = local(1, piece(side_col, side_row), picked.at[2, chip])
    scatter = []
    for dx, dz in plane:
        tx = wrapped("x", x, dx, 4)
        tz = wrapped("z_lo", z_lo, 2 if dz is far else dz % 4, 4)
        row = tz * (1 - core) + tx * core
        col = tx * (1 - core) + tz * core
        target = device(dx=dx, dz=dz)
        scatter.append(go(remote(piece(row, col), picked.at[0, chip], target)))
        scatter.append(go(remote(piece(col, row), picked.at[2, chip], target)))

    for copy in (own_p, own_o, own_a, own_b):
        copy.wait()
    for copy in scatter:
        copy.wait_recv()
    to_sibling = go(remote(picked.at[2], picked.at[1], sibling))
    wanted = []
    for p in range(NB):
        owner = jnp.int32(0)
        for b in range(NB):
            owner += jnp.where(pattern[core, b] == p, owners[core * NB + b], 0)
        wanted.append((jnp.where(lax.rem(owner, 2) == core, 0, 1), lax.div(owner, 2)))
    to_sibling.wait_recv()
    for p in range(NB):
        bases[p, side_col, side_row, 0] = picked[wanted[p]]

    def unit(row, col, quarters, half=None):
        some = pl.ds(0, NB) if half is None else pl.ds(half * (NB // 2), NB // 2)
        place = wrapped("col", side_col, col % 4, 4), wrapped("row", side_row, row % 4, 4)
        return bases.at[some, place[0], place[1], pl.ds(*quarters)]

    def send(ref, target):
        return go(remote(ref, ref, target))

    own, rest = (0, 1), (1, 3)
    over_rows, over_cols, far_cols = {}, {}, {}

    def both_ways(row, part):
        over_cols[row, part] = (send(unit(row, 0, part), along_col(1)), send(unit(row, 0, part), along_col(-1)))

    def have_own(row):
        over_rows[row] = [
            go(remote(unit(row, 0, own), unit(row, 0, (4 - dy, 1)), device(dy=dy))) for dy in (1, 3, 2)]
        both_ways(row, own)

    def have_rest(row):
        for copy in over_rows[row]:
            copy.wait_recv()
        both_ways(row, rest)

    def pass_on(row, part):
        up, down = over_cols[row, part]
        up.wait_recv()
        first = send(unit(row, -1, part, 0), along_col(1))
        down.wait_recv()
        second = send(unit(row, 1, part, 1), along_col(-1))
        far_cols[row, part] = (first, second)

    rows_up = send(unit(0, 0, own), along_row(1))
    rows_down = send(unit(0, 0, own), along_row(-1))
    have_own(0)
    cross_values = remote(tokens, theirs, sibling)
    cross_outgrads = remote(outgrads, theirs, sibling, again=True)

    @pl.when(core == 0)
    def _():
        cross_values.start()

    @pl.when(core == 1)
    def _():
        cross_outgrads.start()

    pending.append(cross_values)

    z_parts = []

    def partial_sum(block):
        if block == 0:
            own_g.wait()
        for copy in quarters[block]:
            copy.wait_recv()
        total = own_grads[block].astype(jnp.float32)
        for j in range(3):
            total += grad_in[j, block].astype(jnp.float32)
        part_out[block] = total.astype(jnp.bfloat16)
        z_parts.append(go(remote(part_out.at[block], part_in.at[block], device(dz=4))))

    rows_up.wait_recv()
    rows_up_far = send(unit(-1, 0, own, 0), along_row(1))
    rows_down.wait_recv()
    rows_down_far = send(unit(1, 0, own, 1), along_row(-1))
    have_own(-1)
    have_own(1)
    pass_on(0, own)
    have_rest(0)
    rows_up_far.wait_recv()
    rows_down_far.wait_recv()
    have_own(2)
    quarters.append(send_quarters(1))
    pass_on(-1, own)
    pass_on(1, own)
    partial_sum(0)
    have_rest(-1)
    pass_on(0, rest)
    have_rest(1)
    pass_on(2, own)
    have_rest(2)

    own_values = pltpu.make_async_copy(tokens, mine, local_sems.at[3])
    own_values.wait()
    cross_values.wait_recv()

    turned = [lax.rem(k + 4 - y, 4) for k in range(4)]

    def columns_of(p, place):
        return jnp.concatenate([bases[p, place, row, turn] for row in range(RING) for turn in turned], axis=0)

    def project(*cols):
        places = [wrapped("col", side_col, col % 4, 4) for col in cols]
        width = PIECE * len(cols)

        def one(p, sums):
            weights = jnp.concatenate([columns_of(p, place) for place in places], axis=1)
            block = values[:, pl.ds(pl.multiple_of(p * BS, BS), BS)]
            out = jnp.dot(block, weights, preferred_element_type=jnp.float32)
            total = jnp.sum((out * out).reshape(2 * tokens_here // 8, 8, width), axis=0)
            here = lax.broadcasted_iota(jnp.int32, (NB, width), 0) == p
            return jnp.where(here, jnp.sum(total, axis=0, keepdims=True), sums)

        sums = lax.fori_loop(0, NB, one, jnp.zeros((NB, width), jnp.float32), unroll=4)
        for n, place in enumerate(places):
            columns = pl.ds(pl.multiple_of(place * PIECE, PIECE), PIECE)
            eig[:, columns] = sums[:, n * PIECE:(n + 1) * PIECE]

    pass_on(-1, rest)
    project(0)
    pass_on(1, rest)
    pass_on(2, rest)
    project(-1, 1)
    partial_sum(1)

    own_rows = pl.ds(pl.multiple_of(y * PIECE, PIECE), PIECE)
    whole = []

    def whole_sum(block):
        z_parts[block].wait_recv()
        total = part_out[block].astype(jnp.float32) + part_in[block].astype(jnp.float32)
        summed[block, own_rows] = total.astype(jnp.bfloat16)
        ref = summed.at[block, own_rows]
        whole.extend([go(remote(ref, ref, device(dy=dy))) for dy in (1, 3, 2)])

    early = [copy for copy in pending if all(copy is not part for part in z_parts)]
    pending[:] = list(z_parts)
    whole_sum(0)
    for copies in far_cols.values():
        for copy in copies:
            copy.wait_recv()
    project(2)

    eig_x[x] = eig[...]
    over_x = [go(remote(eig, eig_x.at[x], device(dx=dx))) for dx in (1, 3, 2)]

    whole_sum(1)

    for copy in early:
        copy.wait_send()

    out_place = z_lo * 2 + lax.div(x, 2)
    in_place = lax.rem(x, 2) * 4
    one_basis = remote(bases.at[out_place], bases.at[NB], sibling)
    two_bases = remote(bases.at[pl.ds(in_place, 2)], bases.at[pl.ds(NB, 2)], sibling)

    @pl.when(core == 0)
    def _():
        one_basis.start()

    @pl.when(core == 1)
    def _():
        two_bases.start()

    for copy in over_x:
        copy.wait_recv()
    eig_y[y] = (eig_x[0] + eig_x[1]) + (eig_x[2] + eig_x[3])
    over_y = [go(remote(eig_y.at[y], eig_y.at[y], device(dy=dy))) for dy in (1, 3, 2)]

    @pl.when(core == 0)
    def _():
        two_bases.wait_recv()
        one_basis.wait_send()

    @pl.when(core == 1)
    def _():
        one_basis.wait_recv()
        two_bases.wait_send()

    for copy in over_y:
        copy.wait_recv()
    eig_z[z] = (eig_y[0] + eig_y[1]) + (eig_y[2] + eig_y[3])
    over_z = [go(remote(eig_z.at[z], eig_z.at[z], device(dz=dz))) for dz in (1, -1, 2, -2, 3, -3, 4)]

    out_basis = out_place * (1 - core) + NB * core

    def in_basis(j):
        return (NB + j) * (1 - core) + (in_place + 2 + j) * core

    def basis(place):
        return jnp.concatenate([columns_of(place, col) for col in range(RING)], axis=1)

    for copy in whole:
        copy.wait_recv()

    def rotate(j, _):
        halfway = lax.dot_general(basis(out_basis), summed[j], (((0,), (0,)), ((), ())),
                                  preferred_element_type=jnp.float32).astype(jnp.bfloat16)
        rotated[j] = jnp.dot(halfway, basis(in_basis(j)), preferred_element_type=jnp.float32)
        return 0

    lax.fori_loop(0, 2, rotate, 0)
    flush_later = list(pending)
    pending.clear()
    for copy in over_z:
        copy.wait_recv()
    total = (eig_z[0] + eig_z[1]) + (eig_z[2] + eig_z[3])
    total += (eig_z[4] + eig_z[5]) + (eig_z[6] + eig_z[7])
    both[core] = total / token_count
    across = go(remote(both.at[core], both.at[core], sibling))
    across.wait_recv()

    for s in range(2):
        for b in range(NB):
            eigen_out[s * NB + b: s * NB + b + 1, :] = both[s, pl.ds(pattern[s, b], 1), :]

    out_scale = both[0, pl.ds(out_place, 1), :].reshape(BS, 1)

    def finish(j, _):
        in_scale = both[1, pl.ds(in_place + 2 * core + j, 1), :]
        scaled = (rotated[j] / (out_scale * in_scale + DAMPING)).astype(jnp.bfloat16)
        returned = jnp.dot(basis(out_basis), scaled, preferred_element_type=jnp.float32).astype(jnp.bfloat16)
        precond[j] = lax.dot_general(returned, basis(in_basis(j)), (((1,), (1,)), ((), ())),
                                     preferred_element_type=jnp.float32).astype(jnp.bfloat16)
        return 0

    lax.fori_loop(0, 2, finish, 0)
    flush()
    for copy in flush_later:
        copy.wait_send()


def local(token_total, tokens, outgrads, grad_parts, basis_slots, pattern, owners):
    here = tokens.shape[0]
    bf16, f32 = jnp.bfloat16, jnp.float32
    anywhere = pl.BlockSpec(memory_space=pl.ANY)
    vmem = pl.BlockSpec(memory_space=pltpu.VMEM)

    def body(*refs):
        kernel(float(token_total), *refs)

    operands = (pattern, owners, tokens, outgrads, grad_parts, basis_slots.reshape(RING, PIECE, BS))
    return pl.pallas_call(
        body,
        out_shape=(jax.ShapeDtypeStruct((2, BS, BS), bf16), jax.ShapeDtypeStruct((2 * NB, BS), f32)),
        in_specs=[anywhere] * 6,
        out_specs=(vmem, vmem),
        scratch_shapes=[
            pltpu.SMEM((2, NB), jnp.int32),
            pltpu.SMEM((2 * NB,), jnp.int32),
            pltpu.VMEM((RING, ROWS, BS), bf16),
            pltpu.VMEM((2 * here, NB * BS), bf16),
            pltpu.VMEM((NB + 2, RING, RING, RING, ROWS, PIECE), bf16),
            pltpu.VMEM((3, 16, ROWS, PIECE), bf16),
            pltpu.VMEM((2, PIECE, BS), bf16),
            pltpu.VMEM((3, 2, PIECE, BS), bf16),
            pltpu.VMEM((2, PIECE, BS), bf16),
            pltpu.VMEM((2, PIECE, BS), bf16),
            pltpu.VMEM((2, BS, BS), bf16),
            pltpu.VMEM((2, BS, BS), f32),
            pltpu.VMEM((NB, BS), f32),
            pltpu.VMEM((4, NB, BS), f32),
            pltpu.VMEM((4, NB, BS), f32),
            pltpu.VMEM((8, NB, BS), f32),
            pltpu.VMEM((2, NB, BS), f32),
            pltpu.SemaphoreType.DMA((N_SEMS,)),
            pltpu.SemaphoreType.DMA((N_SEMS,)),
            pltpu.SemaphoreType.DMA((7,)),
        ],
        compiler_params=pltpu.CompilerParams(
            collective_id=0, has_side_effects=True, vmem_limit_bytes=48 * 2 ** 20),
    )(*[pltpu.with_memory_space_constraint(operand, pltpu.HBM) for operand in operands])


def solution(mesh):
    placed = (
        P(("dp", "mp"), None),
        P(("dp", "mp"), None),
        P("dp", "mp", None, None),
        P("mp", None, None),
        P(),
        P(),
    )

    def whole(tokens, *rest):
        total = tokens.shape[0]
        return jax.shard_map(
            lambda *args: local(total, *args), mesh=mesh, in_specs=placed,
            out_specs=(P("mp", None, None), P()), check_vma=False)(tokens, *rest)

    return whole
```

```python
import jax
import jax.numpy as jnp
from jax import lax
from jax.experimental import pallas as pl
from jax.experimental.pallas import tpu as pltpu
from jax.sharding import PartitionSpec as P

DAMPING = 0.5
NB = 8
BS = 512
RING = 4
PIECE = BS // RING
ROWS = PIECE // RING
MESH = pl.DeviceIdType.MESH
N_SEMS = 128


class Far:
    def __init__(self, sign):
        self.sign = sign

    def __neg__(self):
        return Far(-self.sign)


def kernel(token_count, pattern_in, owners_in, tokens, outgrads, grads, slot, precond, eigen_out,
           pattern, owners, slot_quarter, values, bases, picked, own_grads, grad_in, part_out, part_in, summed, rotated,
           eig, eig_x, eig_y, eig_z, both, send_sems, recv_sems, local_sems):
    dp, mp = lax.axis_index("dp"), lax.axis_index("mp")
    y, z_hi = lax.div(dp, 2), lax.rem(dp, 2)
    core, chip = lax.rem(mp, 2), lax.div(mp, 2)
    x, z_lo = lax.rem(chip, RING), lax.div(chip, RING)
    z = z_hi * RING + z_lo
    known = {}

    def wrapped(name, value, delta, size):
        if (name, delta) not in known:
            known[name, delta] = lax.rem(value + (delta + size), size) if delta else value
        return known[name, delta]

    def mp_part(dx, dz):
        if ("mp", dx, dz) not in known:
            known["mp", dx, dz] = wrapped("z_lo", z_lo, dz % 4, 4) * 8 + wrapped("x", x, dx % 4, 4) * 2
        return known["mp", dx, dz]

    def dp_part(dy, dz):
        if ("dp", dy, dz) not in known:
            known["dp", dy, dz] = wrapped("y", y, dy % 4, 4) * 2 + lax.div(wrapped("z", z, dz % 8, 8), 4)
        return known["dp", dy, dz]
    side_row = z_lo * (1 - core) + x * core
    side_col = x * (1 - core) + z_lo * core

    def device(dx=0, dy=0, dz=0, dc=0):
        if isinstance(dz, Far):
            first, second = device(dx, dy, 2 * dz.sign, dc), device(dx, dy, -2 * dz.sign, dc)
            return tuple(a + (b - a) * core for a, b in zip(first, second))
        return (dp_part(dy, dz), mp_part(dx, dz) + (core if dc == 0 else 1 - core))

    def along(d):
        if ("along", d) not in known:
            over_x, over_z = device(dx=d), device(dz=d)
            known["along", d] = (
                tuple(b + (a - b) * core for a, b in zip(over_x, over_z)),
                tuple(a + (b - a) * core for a, b in zip(over_x, over_z)))
        return known["along", d]

    def along_row(d):
        return along(d)[0]

    def along_col(d):
        return along(d)[1]

    sibling = device(dc=1)
    count = [0]
    pending = []

    def remote(src, dst, target, again=False):
        if not again:
            count[0] += 1
        n = count[0]
        return pltpu.make_async_remote_copy(
            src_ref=src, dst_ref=dst, send_sem=send_sems.at[n], recv_sem=recv_sems.at[n],
            device_id=target, device_id_type=MESH)

    def go(copy):
        copy.start()
        pending.append(copy)
        return copy

    def flush():
        for copy in pending:
            copy.wait_send()
        pending.clear()

    far = Far(1)
    plane = [(dx, dz) for dz in (far, 1, -1, 0) for dx in (2, 1, 3, 0) if dx or dz != 0]
    hops = {0: 0, 1: 1, -1: 1, 2: 2, 3: 1, far: 2}
    plane.sort(key=lambda step: -hops[step[0]] - hops[step[1]])
    offsets = [dict(dx=dx, dz=dz) for dx, dz in plane]
    offsets += [dict(dz=-far), dict(dz=3), dict(dz=-3), dict(dz=4)]
    offsets += [dict(dy=1), dict(dy=3), dict(dy=2)]
    offsets += [dict(dc=1)]

    def local(n, src, dst):
        copy = pltpu.make_async_copy(src, dst, local_sems.at[n])
        copy.start()
        return copy

    tokens_here = tokens.shape[0]
    mine = values.at[pl.ds(0, tokens_here)]
    theirs = values.at[pl.ds(tokens_here, tokens_here)]

    def piece(row, col):
        return slot_quarter.at[row, :, pl.ds(pl.multiple_of(col * PIECE, PIECE), PIECE)]

    barrier = pltpu.get_barrier_semaphore()
    for off in offsets:
        back = {k: -v for k, v in off.items()}
        pl.semaphore_signal(barrier, inc=1, device_id=device(**back), device_id_type=MESH)
    own_p = local(4, pattern_in, pattern)
    own_o = local(5, owners_in, owners)
    own_s = local(6, slot.at[:, pl.ds(pl.multiple_of(y * ROWS, ROWS), ROWS)], slot_quarter)
    own_g = local(2, grads.at[0, :, pl.ds(pl.multiple_of(y * PIECE, PIECE), PIECE)], own_grads)

    @pl.when(core == 0)
    def _():
        pltpu.make_async_copy(outgrads, mine, local_sems.at[3]).start()

    @pl.when(core == 1)
    def _():
        pltpu.make_async_copy(tokens, mine, local_sems.at[3]).start()

    pl.semaphore_wait(barrier, len(offsets))

    def send_quarters(block):
        sent = []
        for j, dy in enumerate((1, 3, 2)):
            ty = wrapped("y", y, dy, 4)
            src = grads.at[0, block, pl.ds(pl.multiple_of(ty * PIECE, PIECE), PIECE)]
            sent.append(go(remote(src, grad_in.at[j, block], device(dy=dy))))
        return sent

    quarters = [send_quarters(0)]

    own_s.wait()
    own_a = local(0, piece(side_row, side_col), picked.at[0, chip])
    own_b = local(1, piece(side_col, side_row), picked.at[2, chip])
    scatter = []
    for dx, dz in plane:
        tx = wrapped("x", x, dx, 4)
        tz = wrapped("z_lo", z_lo, 2 if dz is far else dz % 4, 4)
        row = tz * (1 - core) + tx * core
        col = tx * (1 - core) + tz * core
        target = device(dx=dx, dz=dz)
        scatter.append(go(remote(piece(row, col), picked.at[0, chip], target)))
        scatter.append(go(remote(piece(col, row), picked.at[2, chip], target)))

    for copy in (own_p, own_o, own_a, own_b):
        copy.wait()
    for copy in scatter:
        copy.wait_recv()
    to_sibling = go(remote(picked.at[2], picked.at[1], sibling))
    wanted = []
    for p in range(NB):
        owner = jnp.int32(0)
        for b in range(NB):
            owner += jnp.where(pattern[core, b] == p, owners[core * NB + b], 0)
        wanted.append((jnp.where(lax.rem(owner, 2) == core, 0, 1), lax.div(owner, 2)))
    to_sibling.wait_recv()
    for p in range(NB):
        bases[p, side_col, side_row, 0] = picked[wanted[p]]

    def unit(row, col, quarters, half=None):
        some = pl.ds(0, NB) if half is None else pl.ds(half * (NB // 2), NB // 2)
        place = wrapped("col", side_col, col % 4, 4), wrapped("row", side_row, row % 4, 4)
        return bases.at[some, place[0], place[1], pl.ds(*quarters)]

    def send(ref, target):
        return go(remote(ref, ref, target))

    own, rest = (0, 1), (1, 3)
    over_rows, over_cols, far_cols = {}, {}, {}

    def both_ways(row, part):
        over_cols[row, part] = (send(unit(row, 0, part), along_col(1)), send(unit(row, 0, part), along_col(-1)))

    def have_own(row):
        over_rows[row] = [
            go(remote(unit(row, 0, own), unit(row, 0, (4 - dy, 1)), device(dy=dy))) for dy in (1, 3, 2)]
        both_ways(row, own)

    def have_rest(row):
        for copy in over_rows[row]:
            copy.wait_recv()
        both_ways(row, rest)

    def pass_on(row, part):
        up, down = over_cols[row, part]
        up.wait_recv()
        first = send(unit(row, -1, part, 0), along_col(1))
        down.wait_recv()
        second = send(unit(row, 1, part, 1), along_col(-1))
        far_cols[row, part] = (first, second)

    rows_up = send(unit(0, 0, own), along_row(1))
    rows_down = send(unit(0, 0, own), along_row(-1))
    have_own(0)
    cross_values = remote(tokens, theirs, sibling)
    cross_outgrads = remote(outgrads, theirs, sibling, again=True)

    @pl.when(core == 0)
    def _():
        cross_values.start()

    @pl.when(core == 1)
    def _():
        cross_outgrads.start()

    pending.append(cross_values)

    z_parts = []

    def partial_sum(block):
        if block == 0:
            own_g.wait()
        for copy in quarters[block]:
            copy.wait_recv()
        total = own_grads[block].astype(jnp.float32)
        for j in range(3):
            total += grad_in[j, block].astype(jnp.float32)
        part_out[block] = total.astype(jnp.bfloat16)
        z_parts.append(go(remote(part_out.at[block], part_in.at[block], device(dz=4))))

    rows_up.wait_recv()
    rows_up_far = send(unit(-1, 0, own, 0), along_row(1))
    rows_down.wait_recv()
    rows_down_far = send(unit(1, 0, own, 1), along_row(-1))
    have_own(-1)
    have_own(1)
    pass_on(0, own)
    have_rest(0)
    rows_up_far.wait_recv()
    rows_down_far.wait_recv()
    have_own(2)
    quarters.append(send_quarters(1))
    pass_on(-1, own)
    pass_on(1, own)
    partial_sum(0)
    have_rest(-1)
    pass_on(0, rest)
    have_rest(1)
    pass_on(2, own)
    have_rest(2)

    own_values = pltpu.make_async_copy(tokens, mine, local_sems.at[3])
    own_values.wait()
    cross_values.wait_recv()

    turned = [lax.rem(k + 4 - y, 4) for k in range(4)]

    def columns_of(p, place):
        return jnp.concatenate([bases[p, place, row, turn] for row in range(RING) for turn in turned], axis=0)

    def project(*cols):
        places = [wrapped("col", side_col, col % 4, 4) for col in cols]
        width = PIECE * len(cols)

        def one(p, sums):
            weights = jnp.concatenate([columns_of(p, place) for place in places], axis=1)
            block = values[:, pl.ds(pl.multiple_of(p * BS, BS), BS)]
            out = jnp.dot(block, weights, preferred_element_type=jnp.float32)
            total = jnp.sum((out * out).reshape(2 * tokens_here // 8, 8, width), axis=0)
            here = lax.broadcasted_iota(jnp.int32, (NB, width), 0) == p
            return jnp.where(here, jnp.sum(total, axis=0, keepdims=True), sums)

        sums = lax.fori_loop(0, NB, one, jnp.zeros((NB, width), jnp.float32), unroll=4)
        for n, place in enumerate(places):
            columns = pl.ds(pl.multiple_of(place * PIECE, PIECE), PIECE)
            eig[:, columns] = sums[:, n * PIECE:(n + 1) * PIECE]

    pass_on(-1, rest)
    pass_on(1, rest)
    pass_on(2, rest)
    partial_sum(1)
    project(-1, 1)

    own_rows = pl.ds(pl.multiple_of(y * PIECE, PIECE), PIECE)
    whole = []

    def whole_sum(block):
        z_parts[block].wait_recv()
        total = part_out[block].astype(jnp.float32) + part_in[block].astype(jnp.float32)
        summed[block, own_rows] = total.astype(jnp.bfloat16)
        ref = summed.at[block, own_rows]
        whole.extend([go(remote(ref, ref, device(dy=dy))) for dy in (1, 3, 2)])

    early = [copy for copy in pending if all(copy is not part for part in z_parts)]
    pending[:] = list(z_parts)
    whole_sum(0)
    for copies in far_cols.values():
        for copy in copies:
            copy.wait_recv()
    project(0, 2)

    eig_x[x] = eig[...]
    over_x = [go(remote(eig, eig_x.at[x], device(dx=dx))) for dx in (1, 3, 2)]

    out_place = z_lo * 2 + lax.div(x, 2)
    in_place = lax.rem(x, 2) * 4
    one_basis = remote(bases.at[out_place], bases.at[NB], sibling)
    two_bases = remote(bases.at[pl.ds(in_place, 2)], bases.at[pl.ds(NB, 2)], sibling)

    @pl.when(core == 0)
    def _():
        one_basis.start()

    @pl.when(core == 1)
    def _():
        two_bases.start()

    for copy in early:
        copy.wait_send()
    for copy in over_x:
        copy.wait_recv()
    eig_y[y] = (eig_x[0] + eig_x[1]) + (eig_x[2] + eig_x[3])
    over_y = [go(remote(eig_y.at[y], eig_y.at[y], device(dy=dy))) for dy in (1, 3, 2)]
    whole_sum(1)

    @pl.when(core == 0)
    def _():
        two_bases.wait_recv()
        one_basis.wait_send()

    @pl.when(core == 1)
    def _():
        one_basis.wait_recv()
        two_bases.wait_send()

    out_basis = out_place * (1 - core) + NB * core

    def in_basis(j):
        return (NB + j) * (1 - core) + (in_place + 2 + j) * core

    def basis(place):
        return jnp.concatenate([columns_of(place, col) for col in range(RING)], axis=1)

    def rotate(j):
        for copy in whole[3 * j:3 * j + 3]:
            copy.wait_recv()
        halfway = lax.dot_general(basis(out_basis), summed[j], (((0,), (0,)), ((), ())),
                                  preferred_element_type=jnp.float32).astype(jnp.bfloat16)
        rotated[j] = jnp.dot(halfway, basis(in_basis(j)), preferred_element_type=jnp.float32)

    rotate(0)
    for copy in over_y:
        copy.wait_recv()
    eig_z[z] = (eig_y[0] + eig_y[1]) + (eig_y[2] + eig_y[3])
    over_z = [go(remote(eig_z.at[z], eig_z.at[z], device(dz=dz))) for dz in (1, -1, 2, -2, 3, -3, 4)]

    rotate(1)
    flush_later = list(pending)
    pending.clear()
    for copy in over_z:
        copy.wait_recv()
    total = (eig_z[0] + eig_z[1]) + (eig_z[2] + eig_z[3])
    total += (eig_z[4] + eig_z[5]) + (eig_z[6] + eig_z[7])
    both[core] = total / token_count
    across = go(remote(both.at[core], both.at[core], sibling))
    across.wait_recv()

    for s in range(2):
        for b in range(NB):
            eigen_out[s * NB + b: s * NB + b + 1, :] = both[s, pl.ds(pattern[s, b], 1), :]

    out_scale = both[0, pl.ds(out_place, 1), :].reshape(BS, 1)

    def finish(j, _):
        in_scale = both[1, pl.ds(in_place + 2 * core + j, 1), :]
        scaled = (rotated[j] / (out_scale * in_scale + DAMPING)).astype(jnp.bfloat16)
        returned = jnp.dot(basis(out_basis), scaled, preferred_element_type=jnp.float32).astype(jnp.bfloat16)
        precond[j] = lax.dot_general(returned, basis(in_basis(j)), (((1,), (1,)), ((), ())),
                                     preferred_element_type=jnp.float32).astype(jnp.bfloat16)
        return 0

    lax.fori_loop(0, 2, finish, 0)
    flush()
    for copy in flush_later:
        copy.wait_send()


def local(token_total, tokens, outgrads, grad_parts, basis_slots, pattern, owners):
    here = tokens.shape[0]
    bf16, f32 = jnp.bfloat16, jnp.float32
    anywhere = pl.BlockSpec(memory_space=pl.ANY)
    vmem = pl.BlockSpec(memory_space=pltpu.VMEM)

    def body(*refs):
        kernel(float(token_total), *refs)

    operands = (pattern, owners, tokens, outgrads, grad_parts, basis_slots.reshape(RING, PIECE, BS))
    return pl.pallas_call(
        body,
        out_shape=(jax.ShapeDtypeStruct((2, BS, BS), bf16), jax.ShapeDtypeStruct((2 * NB, BS), f32)),
        in_specs=[anywhere] * 6,
        out_specs=(vmem, vmem),
        scratch_shapes=[
            pltpu.SMEM((2, NB), jnp.int32),
            pltpu.SMEM((2 * NB,), jnp.int32),
            pltpu.VMEM((RING, ROWS, BS), bf16),
            pltpu.VMEM((2 * here, NB * BS), bf16),
            pltpu.VMEM((NB + 2, RING, RING, RING, ROWS, PIECE), bf16),
            pltpu.VMEM((3, 16, ROWS, PIECE), bf16),
            pltpu.VMEM((2, PIECE, BS), bf16),
            pltpu.VMEM((3, 2, PIECE, BS), bf16),
            pltpu.VMEM((2, PIECE, BS), bf16),
            pltpu.VMEM((2, PIECE, BS), bf16),
            pltpu.VMEM((2, BS, BS), bf16),
            pltpu.VMEM((2, BS, BS), f32),
            pltpu.VMEM((NB, BS), f32),
            pltpu.VMEM((4, NB, BS), f32),
            pltpu.VMEM((4, NB, BS), f32),
            pltpu.VMEM((8, NB, BS), f32),
            pltpu.VMEM((2, NB, BS), f32),
            pltpu.SemaphoreType.DMA((N_SEMS,)),
            pltpu.SemaphoreType.DMA((N_SEMS,)),
            pltpu.SemaphoreType.DMA((7,)),
        ],
        compiler_params=pltpu.CompilerParams(
            collective_id=0, has_side_effects=True, vmem_limit_bytes=48 * 2 ** 20),
    )(*[pltpu.with_memory_space_constraint(operand, pltpu.HBM) for operand in operands])


def solution(mesh):
    placed = (
        P(("dp", "mp"), None),
        P(("dp", "mp"), None),
        P("dp", "mp", None, None),
        P("mp", None, None),
        P(),
        P(),
    )

    def whole(tokens, *rest):
        total = tokens.shape[0]
        return jax.shard_map(
            lambda *args: local(total, *args), mesh=mesh, in_specs=placed,
            out_specs=(P("mp", None, None), P()), check_vma=False)(tokens, *rest)

    return whole
```

```python
import jax
import jax.numpy as jnp
from jax import lax
from jax.experimental import pallas as pl
from jax.experimental.pallas import tpu as pltpu
from jax.sharding import PartitionSpec as P

DAMPING = 0.5
NB = 8
BS = 512
RING = 4
PIECE = BS // RING
ROWS = PIECE // RING
MESH = pl.DeviceIdType.MESH
N_SEMS = 128


class Far:
    def __init__(self, sign):
        self.sign = sign

    def __neg__(self):
        return Far(-self.sign)


def kernel(token_count, pattern_in, owners_in, tokens, outgrads, grads, slot, precond, eigen_out,
           pattern, owners, slot_quarter, values, bases, picked, own_grads, grad_in, part_out, part_in, summed, rotated,
           eig, eig_x, eig_y, eig_z, both, send_sems, recv_sems, local_sems):
    dp, mp = lax.axis_index("dp"), lax.axis_index("mp")
    y, z_hi = lax.div(dp, 2), lax.rem(dp, 2)
    core, chip = lax.rem(mp, 2), lax.div(mp, 2)
    x, z_lo = lax.rem(chip, RING), lax.div(chip, RING)
    z = z_hi * RING + z_lo
    known = {}

    def wrapped(name, value, delta, size):
        if (name, delta) not in known:
            known[name, delta] = lax.rem(value + (delta + size), size) if delta else value
        return known[name, delta]

    def mp_part(dx, dz):
        if ("mp", dx, dz) not in known:
            known["mp", dx, dz] = wrapped("z_lo", z_lo, dz % 4, 4) * 8 + wrapped("x", x, dx % 4, 4) * 2
        return known["mp", dx, dz]

    def dp_part(dy, dz):
        if ("dp", dy, dz) not in known:
            known["dp", dy, dz] = wrapped("y", y, dy % 4, 4) * 2 + lax.div(wrapped("z", z, dz % 8, 8), 4)
        return known["dp", dy, dz]
    side_row = z_lo * (1 - core) + x * core
    side_col = x * (1 - core) + z_lo * core

    def device(dx=0, dy=0, dz=0, dc=0):
        if isinstance(dz, Far):
            first, second = device(dx, dy, 2 * dz.sign, dc), device(dx, dy, -2 * dz.sign, dc)
            return tuple(a + (b - a) * core for a, b in zip(first, second))
        return (dp_part(dy, dz), mp_part(dx, dz) + (core if dc == 0 else 1 - core))

    def along(d):
        if ("along", d) not in known:
            over_x, over_z = device(dx=d), device(dz=d)
            known["along", d] = (
                tuple(b + (a - b) * core for a, b in zip(over_x, over_z)),
                tuple(a + (b - a) * core for a, b in zip(over_x, over_z)))
        return known["along", d]

    def along_row(d):
        return along(d)[0]

    def along_col(d):
        return along(d)[1]

    sibling = device(dc=1)
    count = [0]
    pending = []

    def remote(src, dst, target, again=False):
        if not again:
            count[0] += 1
        n = count[0]
        return pltpu.make_async_remote_copy(
            src_ref=src, dst_ref=dst, send_sem=send_sems.at[n], recv_sem=recv_sems.at[n],
            device_id=target, device_id_type=MESH)

    def go(copy):
        copy.start()
        pending.append(copy)
        return copy

    def flush():
        for copy in pending:
            copy.wait_send()
        pending.clear()

    far = Far(1)
    plane = [(dx, dz) for dz in (far, 1, -1, 0) for dx in (2, 1, 3, 0) if dx or dz != 0]
    hops = {0: 0, 1: 1, -1: 1, 2: 2, 3: 1, far: 2}
    plane.sort(key=lambda step: -hops[step[0]] - hops[step[1]])
    offsets = [dict(dx=dx, dz=dz) for dx, dz in plane]
    offsets += [dict(dz=-far), dict(dz=3), dict(dz=-3), dict(dz=4)]
    offsets += [dict(dy=1), dict(dy=3), dict(dy=2)]
    offsets += [dict(dc=1)]

    def local(n, src, dst):
        copy = pltpu.make_async_copy(src, dst, local_sems.at[n])
        copy.start()
        return copy

    tokens_here = tokens.shape[0]
    mine = values.at[pl.ds(0, tokens_here)]
    theirs = values.at[pl.ds(tokens_here, tokens_here)]

    def piece(row, col):
        return slot_quarter.at[row, :, pl.ds(pl.multiple_of(col * PIECE, PIECE), PIECE)]

    barrier = pltpu.get_barrier_semaphore()
    for off in offsets:
        back = {k: -v for k, v in off.items()}
        pl.semaphore_signal(barrier, inc=1, device_id=device(**back), device_id_type=MESH)
    own_p = local(4, pattern_in, pattern)
    own_o = local(5, owners_in, owners)
    own_s = local(6, slot.at[:, pl.ds(pl.multiple_of(y * ROWS, ROWS), ROWS)], slot_quarter)
    own_g = local(2, grads.at[0, :, pl.ds(pl.multiple_of(y * PIECE, PIECE), PIECE)], own_grads)

    @pl.when(core == 0)
    def _():
        pltpu.make_async_copy(outgrads, mine, local_sems.at[3]).start()

    @pl.when(core == 1)
    def _():
        pltpu.make_async_copy(tokens, mine, local_sems.at[3]).start()

    pl.semaphore_wait(barrier, len(offsets))

    def send_quarters(block):
        sent = []
        for j, dy in enumerate((1, 3, 2)):
            ty = wrapped("y", y, dy, 4)
            src = grads.at[0, block, pl.ds(pl.multiple_of(ty * PIECE, PIECE), PIECE)]
            sent.append(go(remote(src, grad_in.at[j, block], device(dy=dy))))
        return sent

    quarters = [send_quarters(0)]

    own_s.wait()
    own_a = local(0, piece(side_row, side_col), picked.at[0, chip])
    own_b = local(1, piece(side_col, side_row), picked.at[2, chip])
    scatter = []
    for dx, dz in plane:
        tx = wrapped("x", x, dx, 4)
        tz = wrapped("z_lo", z_lo, 2 if dz is far else dz % 4, 4)
        row = tz * (1 - core) + tx * core
        col = tx * (1 - core) + tz * core
        target = device(dx=dx, dz=dz)
        scatter.append(go(remote(piece(row, col), picked.at[0, chip], target)))
        scatter.append(go(remote(piece(col, row), picked.at[2, chip], target)))

    for copy in (own_p, own_o, own_a, own_b):
        copy.wait()
    for copy in scatter:
        copy.wait_recv()
    to_sibling = go(remote(picked.at[2], picked.at[1], sibling))
    wanted = []
    for p in range(NB):
        owner = jnp.int32(0)
        for b in range(NB):
            owner += jnp.where(pattern[core, b] == p, owners[core * NB + b], 0)
        wanted.append((jnp.where(lax.rem(owner, 2) == core, 0, 1), lax.div(owner, 2)))
    to_sibling.wait_recv()
    for p in range(NB):
        bases[p, side_col, side_row, 0] = picked[wanted[p]]

    def unit(row, col, quarters, half=None):
        some = pl.ds(0, NB) if half is None else pl.ds(half * (NB // 2), NB // 2)
        place = wrapped("col", side_col, col % 4, 4), wrapped("row", side_row, row % 4, 4)
        return bases.at[some, place[0], place[1], pl.ds(*quarters)]

    def send(ref, target):
        return go(remote(ref, ref, target))

    own, rest = (0, 1), (1, 3)
    over_rows, over_cols, far_cols = {}, {}, {}

    def both_ways(row, part):
        over_cols[row, part] = (send(unit(row, 0, part), along_col(1)), send(unit(row, 0, part), along_col(-1)))

    def have_own(row):
        over_rows[row] = [
            go(remote(unit(row, 0, own), unit(row, 0, (4 - dy, 1)), device(dy=dy))) for dy in (1, 3, 2)]
        both_ways(row, own)

    def have_rest(row):
        for copy in over_rows[row]:
            copy.wait_recv()
        both_ways(row, rest)

    def pass_on(row, part):
        up, down = over_cols[row, part]
        up.wait_recv()
        first = send(unit(row, -1, part, 0), along_col(1))
        down.wait_recv()
        second = send(unit(row, 1, part, 1), along_col(-1))
        far_cols[row, part] = (first, second)

    rows_up = send(unit(0, 0, own), along_row(1))
    rows_down = send(unit(0, 0, own), along_row(-1))
    have_own(0)
    cross_values = remote(tokens, theirs, sibling)
    cross_outgrads = remote(outgrads, theirs, sibling, again=True)

    @pl.when(core == 0)
    def _():
        cross_values.start()

    @pl.when(core == 1)
    def _():
        cross_outgrads.start()

    pending.append(cross_values)

    z_parts = []

    def partial_sum(block):
        if block == 0:
            own_g.wait()
        for copy in quarters[block]:
            copy.wait_recv()
        total = own_grads[block].astype(jnp.float32)
        for j in range(3):
            total += grad_in[j, block].astype(jnp.float32)
        part_out[block] = total.astype(jnp.bfloat16)
        z_parts.append(go(remote(part_out.at[block], part_in.at[block], device(dz=4))))

    rows_up.wait_recv()
    rows_up_far = send(unit(-1, 0, own, 0), along_row(1))
    rows_down.wait_recv()
    rows_down_far = send(unit(1, 0, own, 1), along_row(-1))
    have_own(-1)
    have_own(1)
    pass_on(0, own)
    have_rest(0)
    rows_up_far.wait_recv()
    rows_down_far.wait_recv()
    have_own(2)
    quarters.append(send_quarters(1))
    pass_on(-1, own)
    pass_on(1, own)
    partial_sum(0)
    have_rest(-1)
    pass_on(0, rest)
    have_rest(1)
    pass_on(2, own)
    have_rest(2)

    own_values = pltpu.make_async_copy(tokens, mine, local_sems.at[3])
    own_values.wait()
    cross_values.wait_recv()

    turned = [lax.rem(k + 4 - y, 4) for k in range(4)]

    def columns_of(p, place):
        return jnp.concatenate([bases[p, place, row, turn] for row in range(RING) for turn in turned], axis=0)

    def project(*cols):
        places = [wrapped("col", side_col, col % 4, 4) for col in cols]
        width = PIECE * len(cols)

        def one(p, sums):
            weights = jnp.concatenate([columns_of(p, place) for place in places], axis=1)
            block = values[:, pl.ds(pl.multiple_of(p * BS, BS), BS)]
            out = jnp.dot(block, weights, preferred_element_type=jnp.float32)
            total = jnp.sum((out * out).reshape(2 * tokens_here // 8, 8, width), axis=0)
            here = lax.broadcasted_iota(jnp.int32, (NB, width), 0) == p
            return jnp.where(here, jnp.sum(total, axis=0, keepdims=True), sums)

        sums = lax.fori_loop(0, NB, one, jnp.zeros((NB, width), jnp.float32), unroll=4)
        for n, place in enumerate(places):
            columns = pl.ds(pl.multiple_of(place * PIECE, PIECE), PIECE)
            eig[:, columns] = sums[:, n * PIECE:(n + 1) * PIECE]

    pass_on(-1, rest)
    pass_on(1, rest)
    pass_on(2, rest)
    partial_sum(1)
    project(-1, 1)

    own_rows = pl.ds(pl.multiple_of(y * PIECE, PIECE), PIECE)
    whole = []

    def whole_sum(block):
        z_parts[block].wait_recv()
        total = part_out[block].astype(jnp.float32) + part_in[block].astype(jnp.float32)
        summed[block, own_rows] = total.astype(jnp.bfloat16)
        ref = summed.at[block, own_rows]
        whole.extend([go(remote(ref, ref, device(dy=dy))) for dy in (1, 3, 2)])

    early = [copy for copy in pending if all(copy is not part for part in z_parts)]
    pending[:] = list(z_parts)
    whole_sum(0)
    for copies in far_cols.values():
        for copy in copies:
            copy.wait_recv()
    project(0, 2)

    eig_x[x] = eig[...]
    over_x = [go(remote(eig, eig_x.at[x], device(dx=dx))) for dx in (2, 1, 3)]

    out_place = z_lo * 2 + lax.div(x, 2)
    in_place = lax.rem(x, 2) * 4
    one_basis = remote(bases.at[out_place], bases.at[NB], sibling)
    two_bases = remote(bases.at[pl.ds(in_place, 2)], bases.at[pl.ds(NB, 2)], sibling)

    @pl.when(core == 0)
    def _():
        one_basis.start()

    @pl.when(core == 1)
    def _():
        two_bases.start()

    for copy in early:
        copy.wait_send()
    for copy in over_x:
        copy.wait_recv()
    eig_y[y] = (eig_x[0] + eig_x[1]) + (eig_x[2] + eig_x[3])
    over_y = [go(remote(eig_y.at[y], eig_y.at[y], device(dy=dy))) for dy in (2, 1, 3)]
    whole_sum(1)

    @pl.when(core == 0)
    def _():
        two_bases.wait_recv()
        one_basis.wait_send()

    @pl.when(core == 1)
    def _():
        one_basis.wait_recv()
        two_bases.wait_send()

    out_basis = out_place * (1 - core) + NB * core

    def in_basis(j):
        return (NB + j) * (1 - core) + (in_place + 2 + j) * core

    def basis(place):
        return jnp.concatenate([columns_of(place, col) for col in range(RING)], axis=1)

    def rotate(j):
        for copy in whole[3 * j:3 * j + 3]:
            copy.wait_recv()
        halfway = lax.dot_general(basis(out_basis), summed[j], (((0,), (0,)), ((), ())),
                                  preferred_element_type=jnp.float32).astype(jnp.bfloat16)
        rotated[j] = jnp.dot(halfway, basis(in_basis(j)), preferred_element_type=jnp.float32)

    rotate(0)
    for copy in over_y:
        copy.wait_recv()
    eig_z[z] = (eig_y[0] + eig_y[1]) + (eig_y[2] + eig_y[3])
    over_z = [go(remote(eig_z.at[z], eig_z.at[z], device(dz=dz))) for dz in (4, 3, -3, 2, -2, 1, -1)]

    rotate(1)
    flush_later = list(pending)
    pending.clear()
    for copy in over_z:
        copy.wait_recv()
    total = (eig_z[0] + eig_z[1]) + (eig_z[2] + eig_z[3])
    total += (eig_z[4] + eig_z[5]) + (eig_z[6] + eig_z[7])
    both[core] = total / token_count
    across = go(remote(both.at[core], both.at[core], sibling))
    across.wait_recv()

    for s in range(2):
        for b in range(NB):
            eigen_out[s * NB + b: s * NB + b + 1, :] = both[s, pl.ds(pattern[s, b], 1), :]

    out_scale = both[0, pl.ds(out_place, 1), :].reshape(BS, 1)

    def finish(j, _):
        in_scale = both[1, pl.ds(in_place + 2 * core + j, 1), :]
        scaled = (rotated[j] / (out_scale * in_scale + DAMPING)).astype(jnp.bfloat16)
        returned = jnp.dot(basis(out_basis), scaled, preferred_element_type=jnp.float32).astype(jnp.bfloat16)
        precond[j] = lax.dot_general(returned, basis(in_basis(j)), (((1,), (1,)), ((), ())),
                                     preferred_element_type=jnp.float32).astype(jnp.bfloat16)
        return 0

    lax.fori_loop(0, 2, finish, 0)
    flush()
    for copy in flush_later:
        copy.wait_send()


def local(token_total, tokens, outgrads, grad_parts, basis_slots, pattern, owners):
    here = tokens.shape[0]
    bf16, f32 = jnp.bfloat16, jnp.float32
    anywhere = pl.BlockSpec(memory_space=pl.ANY)
    vmem = pl.BlockSpec(memory_space=pltpu.VMEM)

    def body(*refs):
        kernel(float(token_total), *refs)

    operands = (pattern, owners, tokens, outgrads, grad_parts, basis_slots.reshape(RING, PIECE, BS))
    return pl.pallas_call(
        body,
        out_shape=(jax.ShapeDtypeStruct((2, BS, BS), bf16), jax.ShapeDtypeStruct((2 * NB, BS), f32)),
        in_specs=[anywhere] * 6,
        out_specs=(vmem, vmem),
        scratch_shapes=[
            pltpu.SMEM((2, NB), jnp.int32),
            pltpu.SMEM((2 * NB,), jnp.int32),
            pltpu.VMEM((RING, ROWS, BS), bf16),
            pltpu.VMEM((2 * here, NB * BS), bf16),
            pltpu.VMEM((NB + 2, RING, RING, RING, ROWS, PIECE), bf16),
            pltpu.VMEM((3, 16, ROWS, PIECE), bf16),
            pltpu.VMEM((2, PIECE, BS), bf16),
            pltpu.VMEM((3, 2, PIECE, BS), bf16),
            pltpu.VMEM((2, PIECE, BS), bf16),
            pltpu.VMEM((2, PIECE, BS), bf16),
            pltpu.VMEM((2, BS, BS), bf16),
            pltpu.VMEM((2, BS, BS), f32),
            pltpu.VMEM((NB, BS), f32),
            pltpu.VMEM((4, NB, BS), f32),
            pltpu.VMEM((4, NB, BS), f32),
            pltpu.VMEM((8, NB, BS), f32),
            pltpu.VMEM((2, NB, BS), f32),
            pltpu.SemaphoreType.DMA((N_SEMS,)),
            pltpu.SemaphoreType.DMA((N_SEMS,)),
            pltpu.SemaphoreType.DMA((7,)),
        ],
        compiler_params=pltpu.CompilerParams(
            collective_id=0, has_side_effects=True, vmem_limit_bytes=48 * 2 ** 20),
    )(*[pltpu.with_memory_space_constraint(operand, pltpu.HBM) for operand in operands])


def solution(mesh):
    placed = (
        P(("dp", "mp"), None),
        P(("dp", "mp"), None),
        P("dp", "mp", None, None),
        P("mp", None, None),
        P(),
        P(),
    )

    def whole(tokens, *rest):
        total = tokens.shape[0]
        return jax.shard_map(
            lambda *args: local(total, *args), mesh=mesh, in_specs=placed,
            out_specs=(P("mp", None, None), P()), check_vma=False)(tokens, *rest)

    return whole
```
